32 devices in a mesh: seq: 4 (over y, core), vocab: 8 (over z, x).
Axes of the slice: x: 2, y: 2, z: 4, core: 2. Of those that a mesh axis runs over, the one named last changes fastest.
Arguments:
- queries: bfloat16 [2048, 2, 2048], P(('seq', 'vocab')), may hold values from -40 to 40
- key_vectors: bfloat16 [2048, 2, 2048], P(('seq', 'vocab')), may hold values from -40 to 40
- value_vectors: bfloat16 [2048, 2, 2048], P(('seq', 'vocab')), may hold values from -18 to 18
- residual: bfloat16 [2048, 2, 2048], P(('seq', 'vocab')), may hold values from -3 to 3
- norm_gain: float32 [2048], replicated, may hold values from 0.1 to 1.9
- head_weight: bfloat16 [2048, 8192], P(None, 'vocab'), may hold values from -0.125 to 0.125
- head_bias: float32 [8192], P('vocab'), may hold values from -6 to 6
- doc_lengths: int32 [2], replicated, may hold values from 1 to 2048, 3072 in all
Outputs:
- pooled: float32 [2, 8192], P(None, 'vocab')
- grad_hidden: bfloat16 [2048, 2, 2048], P(('seq', 'vocab'))
The draws below stay inside these ranges and needn't reach their ends.
Inputs may be any that keep to these rules, and one draw needn't show every extreme that they name: `doc_lengths`: the lengths add up to 3072.
All inputs are finite; a program needn't handle non-finite values.
Results may differ from the reference program's by a relative error of at most 0.018.
Values may be sent and summed in bfloat16 or wider, within the bound.
A program may use at most 128 MiB of HBM per device.

```python
import math
import jax
import jax.numpy as jnp
import numpy as np
from jax import lax

D = 2048
HEADS = 16
HEAD_DIM = 128
DOCS = 2
LENGTH = 2048
VOCAB = 8192


def draw_pair(key):
    key_query, key_key = jax.random.split(jax.random.fold_in(key, 7), 2)
    shape = (LENGTH, DOCS, D)
    query_draw = 1.3 * jax.random.normal(key_query, shape, jnp.float32)
    key_draw = 1.3 * jax.random.normal(key_key, shape, jnp.float32)
    return (jnp.clip(query_draw, -40.0, 40.0), jnp.clip(key_draw, -40.0, 40.0))


def draw_queries(key, part):
    return draw_pair(key)[0].astype(jnp.bfloat16)


def draw_key_vectors(key, part):
    return draw_pair(key)[1].astype(jnp.bfloat16)


def level_of(own_key, dims, cuts, least, largest):
    gain = 1.0
    for position, shards_of in cuts:
        draws = jax.random.uniform(jax.random.fold_in(jax.random.fold_in(own_key, 6), position), (shards_of,), jnp.float32, least / len(cuts), largest / len(cuts))
        gain = gain * jnp.repeat(jnp.exp(draws), dims[position] // shards_of).reshape((-1,) + (1,) * (len(dims) - 1 - position))
    return gain


def split_up(amount, total, reach, skew):
    weights = [(1 << 20) // math.isqrt(rank ** skew) + 1 for rank in range(2, amount + 1)]
    spare, holding = total - reach - (amount - 1), [1] * (amount - 1)
    while spare > 0:
        free = [i for i in range(amount - 1) if holding[i] < reach]
        whole, budget = sum([weights[i] for i in free]), spare
        for i in free:
            more = min(reach - holding[i], max(1, budget * weights[i] // whole), spare)
            holding[i] = holding[i] + more
            spare = spare - more
    return np.array([reach] + holding)


def ragged_sizes(stream_key, number_of, total, limit, skew):
    if number_of == 2:
        one = jax.random.randint(stream_key, (), max(1, total - limit), min(limit, total - 1) + 1)
        return jnp.stack([one, total - one])
    sizes = jnp.asarray(split_up(number_of, total, limit, skew), jnp.int32)
    twos = (number_of - 1) // 2
    giver, receiver = sizes[1:1 + 2 * twos:2], sizes[2:2 + 2 * twos:2]
    room = jnp.minimum(giver - 1, limit - receiver)
    moved = jax.random.randint(jax.random.fold_in(stream_key, 1), (twos,), 0, 1 << 20) % (room + 1)
    sizes = sizes.at[1:1 + 2 * twos:2].set(giver - moved).at[2:2 + 2 * twos:2].set(receiver + moved)
    return sizes[jax.random.permutation(jax.random.fold_in(stream_key, 2), number_of)]


def scatter_about(rng, dims, scale, limit, cuts=(), held_as=jnp.bfloat16):
    drawn = jax.random.normal(rng, dims, jnp.float32) * scale
    if len(cuts) > 0:
        drawn = level_of(rng, dims, cuts, -0.22, 0.18) * drawn
    return jnp.clip(drawn, min=-limit, max=limit).astype(held_as)


def setup_inputs(seed: int = 0) -> dict:
    seeds = jax.random.split(jax.random.key(seed), 9)
    queries = draw_queries(jax.random.fold_in(seeds[8], 71), 0)
    key_vectors = draw_key_vectors(jax.random.fold_in(seeds[8], 71), 0)
    value_vectors = scatter_about(seeds[2], (LENGTH, DOCS, D), 3.0, 18.0, ((0, 32),))
    residual = scatter_about(seeds[3], (LENGTH, DOCS, D), 0.5, 3.0, ((0, 32),))
    norm_gain = jnp.clip(1.0 + 0.18 * jax.random.normal(seeds[4], (D,), jnp.float32), 0.1, 1.9)
    head_weight = scatter_about(seeds[5], (D, VOCAB), D ** -0.5, 0.125, ((1, 8),))
    head_bias = scatter_about(seeds[6], (VOCAB,), 1.0, 6.0, ((0, 8),), jnp.float32)
    doc_lengths = ragged_sizes(seeds[7], DOCS, 3 * DOCS * LENGTH // 4, LENGTH, 0).astype(jnp.int32)
    return dict(queries=queries, key_vectors=key_vectors, value_vectors=value_vectors, residual=residual, norm_gain=norm_gain, head_weight=head_weight, head_bias=head_bias, doc_lengths=doc_lengths)


sharpness = 8.0
flops_weight = 500.0
epsilon = 1e-05

def attend_doc(inputs):
    query_head, key_head, value_head, key_allowed = inputs
    scores = jnp.dot(query_head, key_head.T) / math.sqrt(HEAD_DIM)
    allowed = key_allowed[None, :]
    highest = lax.optimization_barrier(jnp.max(jnp.where(allowed, scores, -1e+30), axis=1, keepdims=True))
    weights = jnp.where(allowed, jnp.exp(scores - highest), 0.0)
    weight_sum = lax.optimization_barrier(jnp.sum(weights, axis=1))
    rounded = weights.astype(jnp.bfloat16).astype(jnp.float32)
    summed = jnp.dot(rounded, value_head)
    return (summed / weight_sum[:, None]).astype(jnp.bfloat16)

def attention_head(queries, key_vectors, value_vectors, key_allowed, head_index):
    offset = (head_index * HEAD_DIM).astype(jnp.int32)
    query_head = jnp.transpose(lax.dynamic_slice_in_dim(queries, offset, HEAD_DIM, 2), (1, 0, 2)).astype(jnp.float32)
    key_head = jnp.transpose(lax.dynamic_slice_in_dim(key_vectors, offset, HEAD_DIM, 2), (1, 0, 2)).astype(jnp.float32)
    value_head = jnp.transpose(lax.dynamic_slice_in_dim(value_vectors, offset, HEAD_DIM, 2), (1, 0, 2)).astype(jnp.float32)
    return lax.map(attend_doc, (query_head, key_head, value_head, key_allowed))

def reference(queries, key_vectors, value_vectors, residual, norm_gain, head_weight, head_bias, doc_lengths):
    slot_index = jnp.arange(LENGTH, dtype=jnp.int32)
    key_allowed = slot_index[None, :] < doc_lengths[:, None]
    per_head = lax.map(lambda head_index: attention_head(queries, key_vectors, value_vectors, key_allowed, head_index), jnp.arange(HEADS, dtype=jnp.int32))
    attended = jnp.transpose(per_head, (2, 1, 0, 3)).reshape(LENGTH, DOCS, D)
    combined = residual.astype(jnp.float32) + attended.astype(jnp.float32)
    inv_rms = lax.rsqrt(lax.optimization_barrier(jnp.mean(combined * combined, axis=2, keepdims=True)) + epsilon)
    hidden = (combined * inv_rms * norm_gain).astype(jnp.bfloat16)
    hidden_docs = jnp.transpose(hidden, (1, 0, 2))

    def boosted_of(hidden_doc, length_doc):
        logits = jnp.dot(hidden_doc, head_weight, preferred_element_type=jnp.float32) + head_bias
        saturated = jnp.log1p(jnp.maximum(logits, 0.0))
        row_allowed = slot_index[:, None] < length_doc
        boosted = jnp.where(row_allowed, jnp.exp(sharpness * saturated), 0.0)
        return (logits, boosted)

    def total_of(inputs):
        hidden_doc, length_doc = inputs
        return lax.optimization_barrier(jnp.sum(boosted_of(hidden_doc, length_doc)[1], axis=0))
    totals = lax.map(total_of, (hidden_docs, doc_lengths))
    pooled = jnp.log(totals / doc_lengths[:, None].astype(jnp.float32)) / sharpness
    usage = lax.optimization_barrier(jnp.mean(pooled, axis=0))
    coefficient = 2.0 * flops_weight / DOCS * usage[None, :] / totals

    def gradient_of(inputs):
        hidden_doc, length_doc, coefficient_doc = inputs
        logits, boosted = boosted_of(hidden_doc, length_doc)
        derivative = jnp.where(logits > 0.0, 1.0 / (1.0 + jnp.maximum(logits, 0.0)), 0.0)
        dlogits = (coefficient_doc[None, :] * boosted * derivative).astype(jnp.bfloat16)
        grad_rows = lax.dot_general(dlogits, head_weight, (((1,), (1,)), ((), ())), preferred_element_type=jnp.float32)
        return grad_rows.astype(jnp.bfloat16)
    grad_docs = lax.map(gradient_of, (hidden_docs, doc_lengths, coefficient))
    grad_hidden = jnp.transpose(grad_docs, (1, 0, 2))
    return (pooled, grad_hidden)
```

```python
import functools
import math

import jax
import jax.numpy as jnp
from jax import lax
from jax.experimental import pallas as pl
from jax.experimental.pallas import tpu as pltpu
from jax.sharding import PartitionSpec as P

HEAD_DIM = 128


sharpness = 8.0
flops_weight = 500.0
epsilon = 1e-05


def place(device, vocab_count):
    return (device // vocab_count, device % vocab_count)


def meet(devices, me, vocab_count):
    barrier = pltpu.get_barrier_semaphore()

    @pl.loop(1, devices)
    def greet(step):
        pl.semaphore_signal(
            barrier,
            inc=1,
            device_id=place((me + step) % devices, vocab_count),
            device_id_type=pl.DeviceIdType.MESH,
        )

    pl.semaphore_wait(barrier, devices - 1)


def attend_kernel(
    devices,
    vocab_count,
    heads,
    chunk_blocks,
    lengths_ref,
    packed_ref,
    residual_ref,
    gain_ref,
    hidden_ref,
    arrived,
    attended,
    returned,
    send_sem,
    recv_sem,
    back_send_sem,
    back_recv_sem,
    own_sem,
):
    me = lax.axis_index("seq") * vocab_count + lax.axis_index("vocab")
    docs_count, tokens_here, _ = hidden_ref.shape
    chunk = chunk_blocks * tokens_here
    length = devices * tokens_here
    meet(devices, me, vocab_count)

    def outgoing(other, source):
        return pltpu.make_async_remote_copy(
            src_ref=packed_ref.at[other],
            dst_ref=arrived.at[source],
            send_sem=send_sem.at[other],
            recv_sem=recv_sem.at[source],
            device_id=place(other, vocab_count),
            device_id_type=pl.DeviceIdType.MESH,
        )

    def back(other, source):
        return pltpu.make_async_remote_copy(
            src_ref=attended.at[other],
            dst_ref=returned.at[source],
            send_sem=back_send_sem.at[other],
            recv_sem=back_recv_sem.at[source],
            device_id=place(other, vocab_count),
            device_id_type=pl.DeviceIdType.MESH,
        )

    @pl.loop(1, devices)
    def send(step):
        outgoing((me + step) % devices, me).start()

    own = pltpu.make_async_copy(packed_ref.at[me], arrived.at[me], own_sem)
    own.start()
    own.wait()

    @pl.loop(1, devices)
    def receive(step):
        other = (me + step) % devices
        outgoing(other, other).wait_recv()

    real = lengths_ref[me // heads]
    slots = lax.broadcasted_iota(jnp.int32, (1, length), 1)
    bias = jnp.where(slots < real, 0.0, -1e30)
    factor = math.log2(math.e) / math.sqrt(HEAD_DIM)
    count = devices // chunk_blocks

    @pl.loop(0, count)
    def attend(step):
        first = ((step + me // chunk_blocks) % count) * chunk_blocks
        query = arrived[pl.ds(first, chunk_blocks), 0].reshape(chunk, HEAD_DIM)
        keys = arrived[:, 1].reshape(length, HEAD_DIM)
        scores = lax.dot_general(
            query, keys, (((1,), (1,)), ((), ())), preferred_element_type=jnp.float32
        )
        scores = scores + bias
        top = jnp.max(scores, axis=1, keepdims=True)
        weights = jnp.exp2((scores - top) * factor)
        total = jnp.sum(weights, axis=1, keepdims=True)
        values = arrived[:, 2].reshape(length, HEAD_DIM)
        summed = jnp.dot(
            weights.astype(jnp.bfloat16), values, preferred_element_type=jnp.float32
        )
        result = (summed / total).astype(jnp.bfloat16)
        attended[pl.ds(first, chunk_blocks)] = result.reshape(
            chunk_blocks, tokens_here, HEAD_DIM
        )
        for block in range(chunk_blocks):
            other = first + block

            @pl.when(other != me)
            def give():
                back(other, me).start()

    keep = pltpu.make_async_copy(attended.at[me], returned.at[me], own_sem)
    keep.start()
    keep.wait()

    @pl.loop(1, devices)
    def finish(step):
        other = (me + step) % devices
        back(other, other).wait_recv()

    for doc in range(docs_count):
        combined = []
        squares = jnp.zeros((tokens_here, HEAD_DIM), jnp.float32)
        for head in range(heads):
            term = residual_ref[doc, :, head * HEAD_DIM : (head + 1) * HEAD_DIM].astype(
                jnp.float32
            ) + returned[doc * heads + head].astype(jnp.float32)
            squares = squares + term * term
            combined.append(term)
        mean = jnp.sum(squares, axis=1, keepdims=True) / (heads * HEAD_DIM)
        inv_rms = lax.rsqrt(mean + epsilon)
        for head in range(heads):
            at = slice(head * HEAD_DIM, (head + 1) * HEAD_DIM)
            hidden_ref[doc, :, at] = (combined[head] * inv_rms * gain_ref[:, at]).astype(
                jnp.bfloat16
            )

    @pl.loop(1, devices)
    def drain(step):
        other = (me + step) % devices
        outgoing(other, me).wait_send()
        back(other, me).wait_send()


def attend_all(queries, key_vectors, value_vectors, residual, norm_gain, doc_lengths):
    tokens_here, docs_count, width = queries.shape
    heads = width // HEAD_DIM
    vocab_count = lax.axis_size("vocab")
    devices = lax.axis_size("seq") * vocab_count
    packed = jnp.stack([queries, key_vectors, value_vectors])
    packed = packed.reshape(3, tokens_here, docs_count, heads, HEAD_DIM)
    packed = packed.transpose(2, 3, 0, 1, 4).reshape(devices, 3, tokens_here, HEAD_DIM)
    vmem = pl.BlockSpec(memory_space=pltpu.VMEM)
    return pl.pallas_call(
        functools.partial(attend_kernel, devices, vocab_count, heads, 4),
        out_shape=jax.ShapeDtypeStruct((docs_count, tokens_here, width), jnp.bfloat16),
        in_specs=[pl.BlockSpec(memory_space=pltpu.SMEM), vmem, vmem, vmem],
        out_specs=vmem,
        scratch_shapes=[
            pltpu.VMEM((devices, 3, tokens_here, HEAD_DIM), jnp.bfloat16),
            pltpu.VMEM((devices, tokens_here, HEAD_DIM), jnp.bfloat16),
            pltpu.VMEM((devices, tokens_here, HEAD_DIM), jnp.bfloat16),
            pltpu.SemaphoreType.DMA((devices,)),
            pltpu.SemaphoreType.DMA((devices,)),
            pltpu.SemaphoreType.DMA((devices,)),
            pltpu.SemaphoreType.DMA((devices,)),
            pltpu.SemaphoreType.DMA,
        ],
        compiler_params=pltpu.CompilerParams(
            collective_id=1, has_side_effects=True, vmem_limit_bytes=40 * 1024 * 1024
        ),
    )(doc_lengths, packed, residual.transpose(1, 0, 2), norm_gain[None, :])


def attend_blocks(
    queries, key_vectors, value_vectors, residual, norm_gain, doc_lengths
):
    tokens_here = queries.shape[0]
    docs_count = queries.shape[1]
    vocab_count = lax.axis_size("vocab")
    query_heads, key_heads, value_heads = (
        lax.all_to_all(queries, "seq", split_axis=2, concat_axis=0, tiled=True),
        lax.all_to_all(key_vectors, "seq", split_axis=2, concat_axis=0, tiled=True),
        lax.all_to_all(value_vectors, "seq", split_axis=2, concat_axis=0, tiled=True),
    )
    block_rows = query_heads.shape[0]
    local_width = query_heads.shape[2]
    local_heads = local_width // HEAD_DIM
    query_split = query_heads.reshape(block_rows, docs_count, local_heads, HEAD_DIM)
    within = jnp.arange(block_rows, dtype=jnp.int32)

    def attend_block(carry, block):
        highest, total, summed = carry
        key_block, value_block, shard = block
        key_split = key_block.reshape(block_rows, docs_count, local_heads, HEAD_DIM)
        value_split = value_block.reshape(block_rows, docs_count, local_heads, HEAD_DIM)
        key_place = (
            within // tokens_here * vocab_count + shard
        ) * tokens_here + within % tokens_here
        allowed = (key_place[None, :] < doc_lengths[:, None])[:, None, None, :]
        scores = jnp.einsum(
            "qbhe,kbhe->bhqk", query_split, key_split, preferred_element_type=jnp.float32
        ) / math.sqrt(HEAD_DIM)
        block_top = jnp.max(jnp.where(allowed, scores, -1e30), axis=3)
        new_top = jnp.maximum(highest, block_top)
        weights = jnp.where(allowed, jnp.exp(scores - new_top[..., None]), 0.0)
        shrink = jnp.exp(highest - new_top)
        total = total * shrink + jnp.sum(weights, axis=3)
        added = jnp.einsum(
            "bhqk,kbhe->qbhe",
            weights.astype(jnp.bfloat16),
            value_split,
            preferred_element_type=jnp.float32,
        )
        summed = summed * jnp.transpose(shrink, (2, 0, 1))[..., None] + added
        return ((new_top, total, summed), None)

    initial = (
        jnp.full((docs_count, local_heads, block_rows), -1e30, jnp.float32),
        jnp.zeros((docs_count, local_heads, block_rows), jnp.float32),
        jnp.zeros((block_rows, docs_count, local_heads, HEAD_DIM), jnp.float32),
    )
    carry = initial
    key_piece = lax.all_gather(key_heads, "vocab", axis=0, tiled=True)
    value_piece = lax.all_gather(value_heads, "vocab", axis=0, tiled=True)
    count = key_piece.shape[0] // block_rows
    key_blocks = key_piece.reshape(count, block_rows, docs_count, local_width)
    value_blocks = value_piece.reshape(count, block_rows, docs_count, local_width)
    shards = jnp.arange(count, dtype=jnp.int32)
    carry, unused = lax.scan(attend_block, carry, (key_blocks, value_blocks, shards))
    highest, total, summed = carry
    attended = (
        (summed / jnp.transpose(total, (2, 0, 1))[..., None])
        .reshape(block_rows, docs_count, local_width)
        .astype(jnp.bfloat16)
    )
    returned = lax.all_to_all(attended, "seq", split_axis=0, concat_axis=2, tiled=True)
    combined = residual.astype(jnp.float32) + returned.astype(jnp.float32)
    inv_rms = lax.rsqrt(jnp.mean(combined * combined, axis=2, keepdims=True) + epsilon)
    hidden = (combined * inv_rms * norm_gain).astype(jnp.bfloat16)
    return hidden


def local(
    queries, key_vectors, value_vectors, residual, norm_gain, head_weight, head_bias, doc_lengths
):
    tokens_here = queries.shape[0]
    docs_count = queries.shape[1]
    vocab_count = lax.axis_size("vocab")
    seq_at = lax.axis_index("seq")
    if lax.axis_size("seq") * vocab_count == docs_count * (queries.shape[2] // HEAD_DIM):
        hidden = attend_all(
            queries, key_vectors, value_vectors, residual, norm_gain, doc_lengths
        ).transpose(1, 0, 2)
    else:
        hidden = attend_blocks(
            queries, key_vectors, value_vectors, residual, norm_gain, doc_lengths
        )
    arrived = lax.all_gather(hidden, "vocab", axis=0, tiled=True)
    row_count = arrived.shape[0]
    flattened = jnp.dot(
        arrived.reshape(row_count * docs_count, arrived.shape[2]),
        head_weight,
        preferred_element_type=jnp.float32,
    )
    logits = flattened.reshape(row_count, docs_count, head_weight.shape[1]) + head_bias
    gathered_rows = logits.shape[0]
    row_index = jnp.arange(gathered_rows, dtype=jnp.int32)
    position = (
        seq_at * vocab_count + row_index // tokens_here
    ) * tokens_here + row_index % tokens_here
    row_allowed = position[:, None] < doc_lengths[None, :]
    saturated = jnp.log1p(jnp.maximum(logits, 0.0))
    boosted = jnp.where(row_allowed[:, :, None], jnp.exp(sharpness * saturated), 0.0)
    partial_sums = jnp.sum(boosted, axis=0)
    lengths_float = doc_lengths[:, None].astype(jnp.float32)
    totals = lax.psum(partial_sums, "seq")
    pooled = jnp.log(totals / lengths_float) / sharpness
    coefficient = 2.0 * flops_weight / docs_count * jnp.mean(pooled, axis=0)[None, :] / totals
    derivative = jnp.where(logits > 0.0, 1.0 / (1.0 + jnp.maximum(logits, 0.0)), 0.0)
    dlogits = (coefficient[None, :, :] * boosted * derivative).astype(jnp.bfloat16)
    flattened = lax.dot_general(
        dlogits.reshape(gathered_rows * docs_count, dlogits.shape[2]),
        head_weight,
        (((1,), (1,)), ((), ())),
        preferred_element_type=jnp.float32,
    )
    own_rows = lax.psum_scatter(
        flattened.reshape(gathered_rows, docs_count, head_weight.shape[0]).astype(jnp.bfloat16),
        "vocab",
        scatter_dimension=0,
        tiled=True,
    )
    return (pooled, own_rows)


def solution(mesh):
    in_specs = (
        P(("seq", "vocab"), None, None),
        P(("seq", "vocab"), None, None),
        P(("seq", "vocab"), None, None),
        P(("seq", "vocab"), None, None),
        P(),
        P(None, "vocab"),
        P("vocab"),
        P(),
    )
    out_specs = (P(None, "vocab"), P(("seq", "vocab"), None, None))
    return jax.shard_map(local, mesh=mesh, in_specs=in_specs, out_specs=out_specs, check_vma=False)
```

```python
import functools
import math

import jax
import jax.numpy as jnp
from jax import lax
from jax.experimental import pallas as pl
from jax.experimental.pallas import tpu as pltpu
from jax.sharding import PartitionSpec as P

HEAD_DIM = 128


sharpness = 8.0
flops_weight = 500.0
epsilon = 1e-05


def place(device, vocab_count):
    return (device // vocab_count, device % vocab_count)


def meet(devices, me, vocab_count):
    barrier = pltpu.get_barrier_semaphore()

    @pl.loop(1, devices)
    def greet(step):
        pl.semaphore_signal(
            barrier,
            inc=1,
            device_id=place((me + step) % devices, vocab_count),
            device_id_type=pl.DeviceIdType.MESH,
        )

    pl.semaphore_wait(barrier, devices - 1)


def attend_kernel(
    devices,
    vocab_count,
    heads,
    chunk_blocks,
    lengths_ref,
    packed_ref,
    residual_ref,
    gain_ref,
    hidden_ref,
    arrived,
    attended,
    returned,
    send_sem,
    recv_sem,
    back_send_sem,
    back_recv_sem,
    own_sem,
):
    me = lax.axis_index("seq") * vocab_count + lax.axis_index("vocab")
    docs_count, tokens_here, _ = hidden_ref.shape
    chunk = chunk_blocks * tokens_here
    length = devices * tokens_here
    meet(devices, me, vocab_count)

    def outgoing(other, source):
        return pltpu.make_async_remote_copy(
            src_ref=packed_ref.at[other],
            dst_ref=arrived.at[source],
            send_sem=send_sem.at[other],
            recv_sem=recv_sem.at[source],
            device_id=place(other, vocab_count),
            device_id_type=pl.DeviceIdType.MESH,
        )

    def back(other, source):
        return pltpu.make_async_remote_copy(
            src_ref=attended.at[other],
            dst_ref=returned.at[source],
            send_sem=back_send_sem.at[other],
            recv_sem=back_recv_sem.at[source],
            device_id=place(other, vocab_count),
            device_id_type=pl.DeviceIdType.MESH,
        )

    @pl.loop(1, devices)
    def send(step):
        outgoing((me + step) % devices, me).start()

    own = pltpu.make_async_copy(packed_ref.at[me], arrived.at[me], own_sem)
    own.start()
    own.wait()

    @pl.loop(1, devices)
    def receive(step):
        other = (me + step) % devices
        outgoing(other, other).wait_recv()

    real = lengths_ref[me // heads]
    slots = lax.broadcasted_iota(jnp.int32, (1, length), 1)
    bias = jnp.where(slots < real, 0.0, -1e30)
    factor = math.log2(math.e) / math.sqrt(HEAD_DIM)
    count = devices // chunk_blocks

    @pl.loop(0, count)
    def attend(step):
        first = ((step + me // chunk_blocks) % count) * chunk_blocks
        query = arrived[pl.ds(first, chunk_blocks), 0].reshape(chunk, HEAD_DIM)
        keys = arrived[:, 1].reshape(length, HEAD_DIM)
        scores = lax.dot_general(
            query, keys, (((1,), (1,)), ((), ())), preferred_element_type=jnp.float32
        )
        scores = scores + bias
        top = jnp.max(scores, axis=1, keepdims=True)
        weights = jnp.exp2((scores - top) * factor)
        total = jnp.sum(weights, axis=1, keepdims=True)
        values = arrived[:, 2].reshape(length, HEAD_DIM)
        summed = jnp.dot(
            weights.astype(jnp.bfloat16), values, preferred_element_type=jnp.float32
        )
        result = (summed / total).astype(jnp.bfloat16)
        attended[pl.ds(first, chunk_blocks)] = result.reshape(
            chunk_blocks, tokens_here, HEAD_DIM
        )
        for block in range(chunk_blocks):
            other = first + block

            @pl.when(other != me)
            def give():
                back(other, me).start()

    keep = pltpu.make_async_copy(attended.at[me], returned.at[me], own_sem)
    keep.start()
    keep.wait()

    @pl.loop(1, devices)
    def finish(step):
        other = (me + step) % devices
        back(other, other).wait_recv()

    for doc in range(docs_count):
        combined = []
        squares = jnp.zeros((tokens_here, HEAD_DIM), jnp.float32)
        for head in range(heads):
            term = residual_ref[doc, :, head * HEAD_DIM : (head + 1) * HEAD_DIM].astype(
                jnp.float32
            ) + returned[doc * heads + head].astype(jnp.float32)
            squares = squares + term * term
            combined.append(term)
        mean = jnp.sum(squares, axis=1, keepdims=True) / (heads * HEAD_DIM)
        inv_rms = lax.rsqrt(mean + epsilon)
        for head in range(heads):
            at = slice(head * HEAD_DIM, (head + 1) * HEAD_DIM)
            hidden_ref[doc, :, at] = (combined[head] * inv_rms * gain_ref[:, at]).astype(
                jnp.bfloat16
            )

    @pl.loop(1, devices)
    def drain(step):
        other = (me + step) % devices
        outgoing(other, me).wait_send()
        back(other, me).wait_send()


def attend_all(queries, key_vectors, value_vectors, residual, norm_gain, doc_lengths):
    tokens_here, docs_count, width = queries.shape
    heads = width // HEAD_DIM
    vocab_count = lax.axis_size("vocab")
    devices = lax.axis_size("seq") * vocab_count
    packed = jnp.stack([queries, key_vectors, value_vectors])
    packed = packed.reshape(3, tokens_here, docs_count, heads, HEAD_DIM)
    packed = packed.transpose(2, 3, 0, 1, 4).reshape(devices, 3, tokens_here, HEAD_DIM)
    vmem = pl.BlockSpec(memory_space=pltpu.VMEM)
    return pl.pallas_call(
        functools.partial(attend_kernel, devices, vocab_count, heads, 4),
        out_shape=jax.ShapeDtypeStruct((docs_count, tokens_here, width), jnp.bfloat16),
        in_specs=[pl.BlockSpec(memory_space=pltpu.SMEM), vmem, vmem, vmem],
        out_specs=vmem,
        scratch_shapes=[
            pltpu.VMEM((devices, 3, tokens_here, HEAD_DIM), jnp.bfloat16),
            pltpu.VMEM((devices, tokens_here, HEAD_DIM), jnp.bfloat16),
            pltpu.VMEM((devices, tokens_here, HEAD_DIM), jnp.bfloat16),
            pltpu.SemaphoreType.DMA((devices,)),
            pltpu.SemaphoreType.DMA((devices,)),
            pltpu.SemaphoreType.DMA((devices,)),
            pltpu.SemaphoreType.DMA((devices,)),
            pltpu.SemaphoreType.DMA,
        ],
        compiler_params=pltpu.CompilerParams(
            collective_id=1, has_side_effects=True, vmem_limit_bytes=40 * 1024 * 1024
        ),
    )(doc_lengths, packed, residual.transpose(1, 0, 2), norm_gain[None, :])


def turn(z, step):
    return (3 * (1 - lax.div(z, 2)), lax.rem(2 + 3 * z, 5), 1 + lax.rem(z, 2), z)[step]


def head_kernel(
    lengths_ref,
    hidden_ref,
    weight_hbm,
    bias_ref,
    pooled_ref,
    grad_ref,
    weight,
    rows,
    logits,
    partials,
    slopes,
    across,
    kept,
    from_side,
    from_line,
    passing,
    weight_sem,
    own_sem,
    row_send,
    row_recv,
    sum_send,
    sum_recv,
    side_send,
    side_recv,
    line_send,
    line_recv,
):
    seq_at = lax.axis_index("seq")
    vocab_at = lax.axis_index("vocab")
    z, x = lax.div(vocab_at, 2), lax.rem(vocab_at, 2)
    docs_count, tokens_here, width = grad_ref.shape
    block_rows = docs_count * tokens_here
    entries = weight.shape[1]
    seq_count = partials.shape[0]
    up, down, side = (seq_at, vocab_at + 2), (seq_at, vocab_at - 2), (seq_at, z * 2 + 1 - x)
    mesh_id = pl.DeviceIdType.MESH

    load = pltpu.make_async_copy(weight_hbm, weight, weight_sem)
    load.start()
    own = pltpu.make_async_copy(hidden_ref, rows.at[vocab_at], own_sem)
    own.start()

    barrier = pltpu.get_barrier_semaphore()
    pl.semaphore_signal(barrier, inc=1, device_id=side, device_id_type=mesh_id)
    for step in range(1, seq_count):
        mate = (lax.rem(seq_at + step, seq_count), vocab_at)
        pl.semaphore_signal(barrier, inc=1, device_id=mate, device_id_type=mesh_id)

    @pl.when(z < 3)
    def greet_up():
        pl.semaphore_signal(barrier, inc=1, device_id=up, device_id_type=mesh_id)

    @pl.when(z > 0)
    def greet_down():
        pl.semaphore_signal(barrier, inc=1, device_id=down, device_id_type=mesh_id)

    pl.semaphore_wait(barrier, seq_count + lax.div(z + 3, 4) + lax.div(6 - z, 4))

    def row_copy(slot, way):
        return pltpu.make_async_remote_copy(
            src_ref=rows.at[slot],
            dst_ref=rows.at[slot],
            send_sem=row_send.at[slot, way],
            recv_sem=row_recv.at[slot],
            device_id=(up, down, side)[way],
            device_id_type=mesh_id,
        )

    def pass_rows(row, act):
        slot = row * 2 + x

        @pl.when(jnp.logical_and(row <= z, z < 3))
        def upward():
            act(row_copy(slot, 0))

        @pl.when(jnp.logical_and(row >= z, z > 0))
        def downward():
            act(row_copy(slot, 1))

        act(row_copy(slot, 2))

    partials[seq_at] = jnp.zeros((docs_count, entries), jnp.float32)
    tile = 256

    def project(slot):
        block = rows[slot]

        @pl.loop(0, entries // tile)
        def columns(step):
            at = pl.ds(pl.multiple_of(step * tile, tile), tile)
            found = (
                jnp.dot(block, weight[:, at], preferred_element_type=jnp.float32)
                + bias_ref[:, at]
            )
            first = (seq_at * 8 + slot) * tokens_here
            place_of = first + lax.broadcasted_iota(jnp.int32, (tokens_here, tile), 0)
            for doc in range(docs_count):
                real = place_of < lengths_ref[doc]
                part = found[doc * tokens_here : (doc + 1) * tokens_here]
                base = 1.0 + jnp.maximum(part, 0.0)
                power = base * base
                power = power * power
                boosted = jnp.where(real, power * power, 0.0)
                total = jnp.sum(boosted, axis=0, keepdims=True)
                partials[seq_at, doc : doc + 1, at] = (
                    partials[seq_at, doc : doc + 1, at] + total
                )
                logits[slot, doc * tokens_here : (doc + 1) * tokens_here, at] = jnp.where(
                    real, part, 0.0
                )

    own.wait()
    pass_rows(z, lambda copy: copy.start())
    load.wait()
    project(vocab_at)
    for step in range(1, 4):
        row, before = turn(z, 3 - step), turn(z, 4 - step)
        row_copy(row * 2 + x, 2).wait_recv()
        pass_rows(row, lambda copy: copy.start())
        project(row * 2 + x)
        row_copy(before * 2 + 1 - x, 2).wait_recv()
        project(before * 2 + 1 - x)
    last = turn(z, 0) * 2 + 1 - x
    row_copy(last, 2).wait_recv()
    project(last)

    def sum_copy(step, source):
        return pltpu.make_async_remote_copy(
            src_ref=partials.at[seq_at],
            dst_ref=partials.at[source],
            send_sem=sum_send.at[step],
            recv_sem=sum_recv.at[source],
            device_id=(lax.rem(seq_at + step, seq_count), vocab_at),
            device_id_type=mesh_id,
        )

    for step in range(1, seq_count):
        sum_copy(step, seq_at).start()
    for step in range(1, seq_count):
        sum_copy(step, lax.rem(seq_at + step, seq_count)).wait_recv()
    totals = partials[0]
    for other in range(1, seq_count):
        totals = totals + partials[other]
    usage = jnp.zeros((1, entries), jnp.float32)
    for doc in range(docs_count):
        length = jnp.full((1, entries), lengths_ref[doc], jnp.int32).astype(jnp.float32)
        pooled = jnp.log(totals[doc : doc + 1] / length) / sharpness
        pooled_ref[doc : doc + 1, :] = pooled
        usage = usage + pooled
    usage = usage / docs_count
    coefficient = [
        2.0 * flops_weight / docs_count * usage / totals[doc : doc + 1]
        for doc in range(docs_count)
    ]

    def slope(slot):
        for doc in range(docs_count):
            part = logits[slot, doc * tokens_here : (doc + 1) * tokens_here]
            base = 1.0 + jnp.maximum(part, 0.0)
            square = base * base
            boosted_slope = square * square * (square * base)
            slopes[doc * tokens_here : (doc + 1) * tokens_here] = jnp.where(
                part > 0.0, coefficient[doc] * boosted_slope, 0.0
            ).astype(jnp.bfloat16)

    def gradient(slot, write):
        slope(slot)

        @pl.loop(0, width // tile)
        def features(step):
            at = pl.ds(pl.multiple_of(step * tile, tile), tile)
            write(
                at,
                lax.dot_general(
                    slopes[...],
                    weight[at, :],
                    (((1,), (1,)), ((), ())),
                    preferred_element_type=jnp.float32,
                ),
            )

    def side_copy(row):
        return pltpu.make_async_remote_copy(
            src_ref=across.at[row],
            dst_ref=from_side.at[row],
            send_sem=side_send.at[row],
            recv_sem=side_recv.at[row],
            device_id=side,
            device_id_type=mesh_id,
        )

    def line_copy(row, way):
        return pltpu.make_async_remote_copy(
            src_ref=passing.at[row],
            dst_ref=from_line.at[way, row],
            send_sem=line_send.at[row],
            recv_sem=line_recv.at[way, row],
            device_id=(up, down)[way],
            device_id_type=mesh_id,
        )

    for step in range(4):
        row = turn(z, step)

        def write_across(at, value):
            across[row, :, at] = value.astype(jnp.bfloat16)

        gradient(row * 2 + 1 - x, write_across)
        side_copy(row).start()

    for step in range(4):
        row = turn(z, step)

        def write_kept(at, value):
            kept[row, :, at] = value

        gradient(row * 2 + x, write_kept)
        side_copy(row).wait_recv()

        @pl.when(jnp.logical_and(row >= z, z > 0))
        def from_below():
            line_copy(row, 0).wait_recv()
            kept[row] = kept[row] + from_line[0, row].astype(jnp.float32)

        @pl.when(jnp.logical_and(row <= z, z < 3))
        def from_above():
            line_copy(row, 1).wait_recv()
            kept[row] = kept[row] + from_line[1, row].astype(jnp.float32)

        total = (kept[row] + from_side[row].astype(jnp.float32)).astype(jnp.bfloat16)
        if step < 3:
            passing[row] = total

            @pl.when(row > z)
            def upward():
                line_copy(row, 0).start()

            @pl.when(row < z)
            def downward():
                line_copy(row, 1).start()

        else:
            grad_ref[...] = total.reshape(docs_count, tokens_here, width)

    for step in range(4):
        row = turn(z, step)
        pass_rows(row, lambda copy: copy.wait_send())
        side_copy(row).wait_send()
        if step < 3:
            line_copy(row, 0).wait_send()
    for step in range(1, seq_count):
        sum_copy(step, seq_at).wait_send()


def head_all(hidden, head_weight, head_bias, doc_lengths):
    docs_count, tokens_here, width = hidden.shape
    entries = head_weight.shape[1]
    block_rows = docs_count * tokens_here
    vocab_count = lax.axis_size("vocab")
    seq_count = lax.axis_size("seq")
    vmem = pl.BlockSpec(memory_space=pltpu.VMEM)
    dma = pltpu.SemaphoreType.DMA
    return pl.pallas_call(
        head_kernel,
        out_shape=(
            jax.ShapeDtypeStruct((docs_count, entries), jnp.float32),
            jax.ShapeDtypeStruct((docs_count, tokens_here, width), jnp.bfloat16),
        ),
        in_specs=[
            pl.BlockSpec(memory_space=pltpu.SMEM),
            vmem,
            pl.BlockSpec(memory_space=pl.ANY),
            vmem,
        ],
        out_specs=(vmem, vmem),
        scratch_shapes=[
            pltpu.VMEM((width, entries), jnp.bfloat16),
            pltpu.VMEM((vocab_count, block_rows, width), jnp.bfloat16),
            pltpu.VMEM((vocab_count, block_rows, entries), jnp.float32),
            pltpu.VMEM((seq_count, docs_count, entries), jnp.float32),
            pltpu.VMEM((block_rows, entries), jnp.bfloat16),
            pltpu.VMEM((4, block_rows, width), jnp.bfloat16),
            pltpu.VMEM((4, block_rows, width), jnp.float32),
            pltpu.VMEM((4, block_rows, width), jnp.bfloat16),
            pltpu.VMEM((2, 4, block_rows, width), jnp.bfloat16),
            pltpu.VMEM((4, block_rows, width), jnp.bfloat16),
            dma,
            dma,
            dma((vocab_count, 3)),
            dma((vocab_count,)),
            dma((seq_count,)),
            dma((seq_count,)),
            dma((4,)),
            dma((4,)),
            dma((4,)),
            dma((2, 4)),
        ],
        compiler_params=pltpu.CompilerParams(
            collective_id=2, has_side_effects=True, vmem_limit_bytes=48 * 1024 * 1024
        ),
    )(doc_lengths, hidden.reshape(block_rows, width), head_weight, head_bias[None, :])


def attend_blocks(
    queries, key_vectors, value_vectors, residual, norm_gain, doc_lengths
):
    tokens_here = queries.shape[0]
    docs_count = queries.shape[1]
    vocab_count = lax.axis_size("vocab")
    query_heads, key_heads, value_heads = (
        lax.all_to_all(queries, "seq", split_axis=2, concat_axis=0, tiled=True),
        lax.all_to_all(key_vectors, "seq", split_axis=2, concat_axis=0, tiled=True),
        lax.all_to_all(value_vectors, "seq", split_axis=2, concat_axis=0, tiled=True),
    )
    block_rows = query_heads.shape[0]
    local_width = query_heads.shape[2]
    local_heads = local_width // HEAD_DIM
    query_split = query_heads.reshape(block_rows, docs_count, local_heads, HEAD_DIM)
    within = jnp.arange(block_rows, dtype=jnp.int32)

    def attend_block(carry, block):
        highest, total, summed = carry
        key_block, value_block, shard = block
        key_split = key_block.reshape(block_rows, docs_count, local_heads, HEAD_DIM)
        value_split = value_block.reshape(block_rows, docs_count, local_heads, HEAD_DIM)
        key_place = (
            within // tokens_here * vocab_count + shard
        ) * tokens_here + within % tokens_here
        allowed = (key_place[None, :] < doc_lengths[:, None])[:, None, None, :]
        scores = jnp.einsum(
            "qbhe,kbhe->bhqk", query_split, key_split, preferred_element_type=jnp.float32
        ) / math.sqrt(HEAD_DIM)
        block_top = jnp.max(jnp.where(allowed, scores, -1e30), axis=3)
        new_top = jnp.maximum(highest, block_top)
        weights = jnp.where(allowed, jnp.exp(scores - new_top[..., None]), 0.0)
        shrink = jnp.exp(highest - new_top)
        total = total * shrink + jnp.sum(weights, axis=3)
        added = jnp.einsum(
            "bhqk,kbhe->qbhe",
            weights.astype(jnp.bfloat16),
            value_split,
            preferred_element_type=jnp.float32,
        )
        summed = summed * jnp.transpose(shrink, (2, 0, 1))[..., None] + added
        return ((new_top, total, summed), None)

    initial = (
        jnp.full((docs_count, local_heads, block_rows), -1e30, jnp.float32),
        jnp.zeros((docs_count, local_heads, block_rows), jnp.float32),
        jnp.zeros((block_rows, docs_count, local_heads, HEAD_DIM), jnp.float32),
    )
    carry = initial
    key_piece = lax.all_gather(key_heads, "vocab", axis=0, tiled=True)
    value_piece = lax.all_gather(value_heads, "vocab", axis=0, tiled=True)
    count = key_piece.shape[0] // block_rows
    key_blocks = key_piece.reshape(count, block_rows, docs_count, local_width)
    value_blocks = value_piece.reshape(count, block_rows, docs_count, local_width)
    shards = jnp.arange(count, dtype=jnp.int32)
    carry, unused = lax.scan(attend_block, carry, (key_blocks, value_blocks, shards))
    highest, total, summed = carry
    attended = (
        (summed / jnp.transpose(total, (2, 0, 1))[..., None])
        .reshape(block_rows, docs_count, local_width)
        .astype(jnp.bfloat16)
    )
    returned = lax.all_to_all(attended, "seq", split_axis=0, concat_axis=2, tiled=True)
    combined = residual.astype(jnp.float32) + returned.astype(jnp.float32)
    inv_rms = lax.rsqrt(jnp.mean(combined * combined, axis=2, keepdims=True) + epsilon)
    hidden = (combined * inv_rms * norm_gain).astype(jnp.bfloat16)
    return hidden


def local(
    queries, key_vectors, value_vectors, residual, norm_gain, head_weight, head_bias, doc_lengths
):
    tokens_here = queries.shape[0]
    docs_count = queries.shape[1]
    vocab_count = lax.axis_size("vocab")
    seq_at = lax.axis_index("seq")
    heads = queries.shape[2] // HEAD_DIM
    if vocab_count == 8 and lax.axis_size("seq") * vocab_count == docs_count * heads:
        hidden = attend_all(
            queries, key_vectors, value_vectors, residual, norm_gain, doc_lengths
        )
        pooled, gradient = head_all(hidden, head_weight, head_bias, doc_lengths)
        return (pooled, gradient.transpose(1, 0, 2))
    hidden = attend_blocks(
        queries, key_vectors, value_vectors, residual, norm_gain, doc_lengths
    )
    arrived = lax.all_gather(hidden, "vocab", axis=0, tiled=True)
    row_count = arrived.shape[0]
    flattened = jnp.dot(
        arrived.reshape(row_count * docs_count, arrived.shape[2]),
        head_weight,
        preferred_element_type=jnp.float32,
    )
    logits = flattened.reshape(row_count, docs_count, head_weight.shape[1]) + head_bias
    gathered_rows = logits.shape[0]
    row_index = jnp.arange(gathered_rows, dtype=jnp.int32)
    position = (
        seq_at * vocab_count + row_index // tokens_here
    ) * tokens_here + row_index % tokens_here
    row_allowed = position[:, None] < doc_lengths[None, :]
    saturated = jnp.log1p(jnp.maximum(logits, 0.0))
    boosted = jnp.where(row_allowed[:, :, None], jnp.exp(sharpness * saturated), 0.0)
    partial_sums = jnp.sum(boosted, axis=0)
    lengths_float = doc_lengths[:, None].astype(jnp.float32)
    totals = lax.psum(partial_sums, "seq")
    pooled = jnp.log(totals / lengths_float) / sharpness
    coefficient = 2.0 * flops_weight / docs_count * jnp.mean(pooled, axis=0)[None, :] / totals
    derivative = jnp.where(logits > 0.0, 1.0 / (1.0 + jnp.maximum(logits, 0.0)), 0.0)
    dlogits = (coefficient[None, :, :] * boosted * derivative).astype(jnp.bfloat16)
    flattened = lax.dot_general(
        dlogits.reshape(gathered_rows * docs_count, dlogits.shape[2]),
        head_weight,
        (((1,), (1,)), ((), ())),
        preferred_element_type=jnp.float32,
    )
    own_rows = lax.psum_scatter(
        flattened.reshape(gathered_rows, docs_count, head_weight.shape[0]).astype(jnp.bfloat16),
        "vocab",
        scatter_dimension=0,
        tiled=True,
    )
    return (pooled, own_rows)


def solution(mesh):
    in_specs = (
        P(("seq", "vocab"), None, None),
        P(("seq", "vocab"), None, None),
        P(("seq", "vocab"), None, None),
        P(("seq", "vocab"), None, None),
        P(),
        P(None, "vocab"),
        P("vocab"),
        P(),
    )
    out_specs = (P(None, "vocab"), P(("seq", "vocab"), None, None))
    return jax.shard_map(local, mesh=mesh, in_specs=in_specs, out_specs=out_specs, check_vma=False)
```

```python
import functools
import math

import jax
import jax.numpy as jnp
from jax import lax
from jax.experimental import pallas as pl
from jax.experimental.pallas import tpu as pltpu
from jax.sharding import PartitionSpec as P

HEAD_DIM = 128


sharpness = 8.0
flops_weight = 500.0
epsilon = 1e-05


def place(device, vocab_count):
    return (device // vocab_count, device % vocab_count)


def meet(devices, me, vocab_count):
    barrier = pltpu.get_barrier_semaphore()

    @pl.loop(1, devices)
    def greet(step):
        pl.semaphore_signal(
            barrier,
            inc=1,
            device_id=place((me + step) % devices, vocab_count),
            device_id_type=pl.DeviceIdType.MESH,
        )

    pl.semaphore_wait(barrier, devices - 1)


def attend_kernel(
    devices,
    vocab_count,
    heads,
    chunk_blocks,
    lengths_ref,
    packed_ref,
    residual_ref,
    gain_ref,
    hidden_ref,
    arrived,
    attended,
    returned,
    send_sem,
    recv_sem,
    back_send_sem,
    back_recv_sem,
    own_sem,
):
    me = lax.axis_index("seq") * vocab_count + lax.axis_index("vocab")
    docs_count, tokens_here, _ = hidden_ref.shape
    chunk = chunk_blocks * tokens_here
    length = devices * tokens_here
    meet(devices, me, vocab_count)

    def outgoing(other, source):
        return pltpu.make_async_remote_copy(
            src_ref=packed_ref.at[other],
            dst_ref=arrived.at[source],
            send_sem=send_sem.at[other],
            recv_sem=recv_sem.at[source],
            device_id=place(other, vocab_count),
            device_id_type=pl.DeviceIdType.MESH,
        )

    def back(other, source):
        return pltpu.make_async_remote_copy(
            src_ref=attended.at[other],
            dst_ref=returned.at[source],
            send_sem=back_send_sem.at[other],
            recv_sem=back_recv_sem.at[source],
            device_id=place(other, vocab_count),
            device_id_type=pl.DeviceIdType.MESH,
        )

    @pl.loop(1, devices)
    def send(step):
        outgoing((me + step) % devices, me).start()

    own = pltpu.make_async_copy(packed_ref.at[me], arrived.at[me], own_sem)
    own.start()
    own.wait()

    @pl.loop(1, devices)
    def receive(step):
        other = (me + step) % devices
        outgoing(other, other).wait_recv()

    real = lengths_ref[me // heads]
    slots = lax.broadcasted_iota(jnp.int32, (1, length), 1)
    bias = jnp.where(slots < real, 0.0, -1e30)
    factor = math.log2(math.e) / math.sqrt(HEAD_DIM)
    count = devices // chunk_blocks

    @pl.loop(0, count)
    def attend(step):
        first = ((step + me // chunk_blocks) % count) * chunk_blocks
        query = arrived[pl.ds(first, chunk_blocks), 0].reshape(chunk, HEAD_DIM)
        keys = arrived[:, 1].reshape(length, HEAD_DIM)
        scores = lax.dot_general(
            query, keys, (((1,), (1,)), ((), ())), preferred_element_type=jnp.float32
        )
        scores = scores + bias
        top = jnp.max(scores, axis=1, keepdims=True)
        weights = jnp.exp2((scores - top) * factor)
        total = jnp.sum(weights, axis=1, keepdims=True)
        values = arrived[:, 2].reshape(length, HEAD_DIM)
        summed = jnp.dot(
            weights.astype(jnp.bfloat16), values, preferred_element_type=jnp.float32
        )
        result = (summed / total).astype(jnp.bfloat16)
        attended[pl.ds(first, chunk_blocks)] = result.reshape(
            chunk_blocks, tokens_here, HEAD_DIM
        )
        for block in range(chunk_blocks):
            other = first + block

            @pl.when(other != me)
            def give():
                back(other, me).start()

    keep = pltpu.make_async_copy(attended.at[me], returned.at[me], own_sem)
    keep.start()
    keep.wait()

    @pl.loop(1, devices)
    def finish(step):
        other = (me + step) % devices
        back(other, other).wait_recv()

    for doc in range(docs_count):
        combined = []
        squares = jnp.zeros((tokens_here, HEAD_DIM), jnp.float32)
        for head in range(heads):
            term = residual_ref[doc, :, head * HEAD_DIM : (head + 1) * HEAD_DIM].astype(
                jnp.float32
            ) + returned[doc * heads + head].astype(jnp.float32)
            squares = squares + term * term
            combined.append(term)
        mean = jnp.sum(squares, axis=1, keepdims=True) / (heads * HEAD_DIM)
        inv_rms = lax.rsqrt(mean + epsilon)
        for head in range(heads):
            at = slice(head * HEAD_DIM, (head + 1) * HEAD_DIM)
            hidden_ref[doc, :, at] = (combined[head] * inv_rms * gain_ref[:, at]).astype(
                jnp.bfloat16
            )

    @pl.loop(1, devices)
    def drain(step):
        other = (me + step) % devices
        outgoing(other, me).wait_send()
        back(other, me).wait_send()


def attend_all(queries, key_vectors, value_vectors, residual, norm_gain, doc_lengths):
    tokens_here, docs_count, width = queries.shape
    heads = width // HEAD_DIM
    vocab_count = lax.axis_size("vocab")
    devices = lax.axis_size("seq") * vocab_count
    packed = jnp.stack([queries, key_vectors, value_vectors])
    packed = packed.reshape(3, tokens_here, docs_count, heads, HEAD_DIM)
    packed = packed.transpose(2, 3, 0, 1, 4).reshape(devices, 3, tokens_here, HEAD_DIM)
    vmem = pl.BlockSpec(memory_space=pltpu.VMEM)
    return pl.pallas_call(
        functools.partial(attend_kernel, devices, vocab_count, heads, 4),
        out_shape=jax.ShapeDtypeStruct((docs_count, tokens_here, width), jnp.bfloat16),
        in_specs=[pl.BlockSpec(memory_space=pltpu.SMEM), vmem, vmem, vmem],
        out_specs=vmem,
        scratch_shapes=[
            pltpu.VMEM((devices, 3, tokens_here, HEAD_DIM), jnp.bfloat16),
            pltpu.VMEM((devices, tokens_here, HEAD_DIM), jnp.bfloat16),
            pltpu.VMEM((devices, tokens_here, HEAD_DIM), jnp.bfloat16),
            pltpu.SemaphoreType.DMA((devices,)),
            pltpu.SemaphoreType.DMA((devices,)),
            pltpu.SemaphoreType.DMA((devices,)),
            pltpu.SemaphoreType.DMA((devices,)),
            pltpu.SemaphoreType.DMA,
        ],
        compiler_params=pltpu.CompilerParams(
            collective_id=1, has_side_effects=True, vmem_limit_bytes=40 * 1024 * 1024
        ),
    )(doc_lengths, packed, residual.transpose(1, 0, 2), norm_gain[None, :])


def turn(z, step):
    return (3 * (1 - lax.div(z, 2)), lax.rem(2 + 3 * z, 5), 1 + lax.rem(z, 2), z)[step]


def head_kernel(
    lengths_ref,
    hidden_ref,
    weight_hbm,
    bias_ref,
    pooled_ref,
    grad_ref,
    weight,
    rows,
    logits,
    partials,
    slopes,
    across,
    kept,
    from_side,
    from_line,
    passing,
    from_partner,
    weight_sem,
    own_sem,
    row_send,
    row_recv,
    sum_send,
    sum_recv,
    side_send,
    side_recv,
    line_send,
    line_recv,
    partner_send,
    partner_recv,
):
    seq_at = lax.axis_index("seq")
    vocab_at = lax.axis_index("vocab")
    z, x = lax.div(vocab_at, 2), lax.rem(vocab_at, 2)
    docs_count, tokens_here, width = grad_ref.shape
    block_rows = docs_count * tokens_here
    entries = weight.shape[1]
    seq_count = partials.shape[0]
    up, down, side = (seq_at, vocab_at + 2), (seq_at, vocab_at - 2), (seq_at, z * 2 + 1 - x)
    partner_row = z + 1 - 2 * lax.rem(z, 2)
    partner = (seq_at, partner_row * 2 + x)
    mesh_id = pl.DeviceIdType.MESH

    load = pltpu.make_async_copy(weight_hbm, weight, weight_sem)
    load.start()
    own = pltpu.make_async_copy(hidden_ref, rows.at[vocab_at], own_sem)
    own.start()

    barrier = pltpu.get_barrier_semaphore()
    pl.semaphore_signal(barrier, inc=1, device_id=side, device_id_type=mesh_id)
    for step in range(1, seq_count):
        mate = (lax.rem(seq_at + step, seq_count), vocab_at)
        pl.semaphore_signal(barrier, inc=1, device_id=mate, device_id_type=mesh_id)

    @pl.when(z < 3)
    def greet_up():
        pl.semaphore_signal(barrier, inc=1, device_id=up, device_id_type=mesh_id)

    @pl.when(z > 0)
    def greet_down():
        pl.semaphore_signal(barrier, inc=1, device_id=down, device_id_type=mesh_id)

    pl.semaphore_wait(barrier, seq_count + lax.div(z + 3, 4) + lax.div(6 - z, 4))

    def row_copy(slot, way, half):
        part = rows.at[slot, pl.ds(half * tokens_here, tokens_here)]
        return pltpu.make_async_remote_copy(
            src_ref=part,
            dst_ref=part,
            send_sem=row_send.at[slot, way, half],
            recv_sem=row_recv.at[slot, half],
            device_id=(up, down, side, partner)[way],
            device_id_type=mesh_id,
        )

    def pass_rows(row, half, act):
        slot = row * 2 + x

        @pl.when(jnp.logical_and(row <= z, z < 3))
        def upward():
            act(row_copy(slot, 0, half))

        @pl.when(jnp.logical_and(row >= z, z > 0))
        def downward():
            act(row_copy(slot, 1, half))

        if half == 0:
            act(row_copy(slot, 2, half))
        else:

            @pl.when(row != partner_row)
            def sideways():
                act(row_copy(slot, 2, half))

    partials[seq_at] = jnp.zeros((docs_count, entries), jnp.float32)
    tile = 256

    def project(slot):
        block = rows[slot]

        @pl.loop(0, entries // tile)
        def columns(step):
            at = pl.ds(pl.multiple_of(step * tile, tile), tile)
            found = (
                jnp.dot(block, weight[:, at], preferred_element_type=jnp.float32)
                + bias_ref[:, at]
            )
            first = (seq_at * 8 + slot) * tokens_here
            place_of = first + lax.broadcasted_iota(jnp.int32, (tokens_here, tile), 0)
            for doc in range(docs_count):
                real = place_of < lengths_ref[doc]
                part = found[doc * tokens_here : (doc + 1) * tokens_here]
                base = 1.0 + jnp.maximum(part, 0.0)
                power = base * base
                power = power * power
                boosted = jnp.where(real, power * power, 0.0)
                total = jnp.sum(boosted, axis=0, keepdims=True)
                partials[seq_at, doc : doc + 1, at] = (
                    partials[seq_at, doc : doc + 1, at] + total
                )
                logits[slot, doc * tokens_here : (doc + 1) * tokens_here, at] = jnp.where(
                    real, part, 0.0
                )

    own.wait()
    for half in range(2):
        pass_rows(z, half, lambda copy: copy.start())
    load.wait()
    project(vocab_at)
    for step in range(1, 4):
        row, before = turn(z, 3 - step), turn(z, 4 - step)
        for half in range(2):
            row_copy(row * 2 + x, 2, half).wait_recv()
            pass_rows(row, half, lambda copy: copy.start())
        if step > 1:
            project(row * 2 + x)
        for half in range(2):
            row_copy(before * 2 + 1 - x, 2, half).wait_recv()
        if step == 1:
            row_copy(before * 2 + 1 - x, 3, 1).start()
            project(row * 2 + x)
        project(before * 2 + 1 - x)
    last = turn(z, 0) * 2 + 1 - x
    for half in range(2):
        row_copy(last, 2, half).wait_recv()
    project(last)

    def sum_copy(step, source):
        return pltpu.make_async_remote_copy(
            src_ref=partials.at[seq_at],
            dst_ref=partials.at[source],
            send_sem=sum_send.at[step],
            recv_sem=sum_recv.at[source],
            device_id=(lax.rem(seq_at + step, seq_count), vocab_at),
            device_id_type=mesh_id,
        )

    for step in range(1, seq_count):
        sum_copy(step, seq_at).start()
    for step in range(1, seq_count):
        sum_copy(step, lax.rem(seq_at + step, seq_count)).wait_recv()
    totals = partials[0]
    for other in range(1, seq_count):
        totals = totals + partials[other]
    usage = jnp.zeros((1, entries), jnp.float32)
    for doc in range(docs_count):
        length = jnp.full((1, entries), lengths_ref[doc], jnp.int32).astype(jnp.float32)
        pooled = jnp.log(totals[doc : doc + 1] / length) / sharpness
        pooled_ref[doc : doc + 1, :] = pooled
        usage = usage + pooled
    usage = usage / docs_count
    coefficient = [
        2.0 * flops_weight / docs_count * usage / totals[doc : doc + 1]
        for doc in range(docs_count)
    ]

    def slope(slot):
        for doc in range(docs_count):
            part = logits[slot, doc * tokens_here : (doc + 1) * tokens_here]
            base = 1.0 + jnp.maximum(part, 0.0)
            square = base * base
            boosted_slope = square * square * (square * base)
            slopes[doc * tokens_here : (doc + 1) * tokens_here] = jnp.where(
                part > 0.0, coefficient[doc] * boosted_slope, 0.0
            ).astype(jnp.bfloat16)

    def gradient(slot, write):
        slope(slot)

        @pl.loop(0, width // tile)
        def features(step):
            at = pl.ds(pl.multiple_of(step * tile, tile), tile)
            write(
                at,
                lax.dot_general(
                    slopes[...],
                    weight[at, :],
                    (((1,), (1,)), ((), ())),
                    preferred_element_type=jnp.float32,
                ),
            )

    def side_copy(row, half):
        part = pl.ds(half * tokens_here, tokens_here)
        return pltpu.make_async_remote_copy(
            src_ref=across.at[row, part],
            dst_ref=from_side.at[row, part],
            send_sem=side_send.at[row, half],
            recv_sem=side_recv.at[row, half],
            device_id=side,
            device_id_type=mesh_id,
        )

    partner_copy = pltpu.make_async_remote_copy(
        src_ref=across.at[partner_row, pl.ds(tokens_here, tokens_here)],
        dst_ref=from_partner,
        send_sem=partner_send,
        recv_sem=partner_recv,
        device_id=partner,
        device_id_type=mesh_id,
    )

    def line_copy(row, way, half):
        part = pl.ds(half * tokens_here, tokens_here)
        return pltpu.make_async_remote_copy(
            src_ref=passing.at[row, part],
            dst_ref=from_line.at[way, row, part],
            send_sem=line_send.at[row, half],
            recv_sem=line_recv.at[way, row, half],
            device_id=(up, down)[way],
            device_id_type=mesh_id,
        )

    for step in range(4):
        row = turn(z, step)

        def write_across(at, value):
            across[row, :, at] = value.astype(jnp.bfloat16)

        gradient(row * 2 + 1 - x, write_across)
        side_copy(row, 0).start()
        if step < 3:

            @pl.when(row == partner_row)
            def by_line():
                partner_copy.start()

            @pl.when(row != partner_row)
            def by_side():
                side_copy(row, 1).start()

    for step in range(4):
        row = turn(z, step)

        def write_kept(at, value):
            kept[row, :, at] = value

        gradient(row * 2 + x, write_kept)
        if step == 0:
            partner_copy.wait_recv()
            late = pl.ds(tokens_here, tokens_here)
            across[z, late] = (
                across[z, late].astype(jnp.float32) + from_partner[...].astype(jnp.float32)
            ).astype(jnp.bfloat16)
            side_copy(z, 1).start()
        for half in range(2):
            part = pl.ds(half * tokens_here, tokens_here)

            @pl.when(jnp.logical_and(row >= z, z > 0))
            def from_below():
                line_copy(row, 0, half).wait_recv()
                kept[row, part] = kept[row, part] + from_line[0, row, part].astype(
                    jnp.float32
                )

            @pl.when(jnp.logical_and(row <= z, z < 3))
            def from_above():
                line_copy(row, 1, half).wait_recv()
                kept[row, part] = kept[row, part] + from_line[1, row, part].astype(
                    jnp.float32
                )

            def add_side():
                side_copy(row, half).wait_recv()
                kept[row, part] = kept[row, part] + from_side[row, part].astype(jnp.float32)

            if half == 0 or step == 3:
                add_side()
            else:
                pl.when(row != partner_row)(add_side)
            total = kept[row, part].astype(jnp.bfloat16)
            if step < 3:
                passing[row, part] = total

                @pl.when(row > z)
                def upward():
                    line_copy(row, 0, half).start()

                @pl.when(row < z)
                def downward():
                    line_copy(row, 1, half).start()

            else:
                grad_ref[half] = total

    for step in range(4):
        row = turn(z, step)
        for half in range(2):
            pass_rows(row, half, lambda copy: copy.wait_send())
            if step < 3:
                line_copy(row, 0, half).wait_send()
        side_copy(row, 0).wait_send()

        @pl.when(row != partner_row)
        def sent():
            side_copy(row, 1).wait_send()

    partner_copy.wait_send()
    row_copy(z * 2 + 1 - x, 3, 1).wait_send()
    for step in range(1, seq_count):
        sum_copy(step, seq_at).wait_send()


def head_all(hidden, head_weight, head_bias, doc_lengths):
    docs_count, tokens_here, width = hidden.shape
    entries = head_weight.shape[1]
    block_rows = docs_count * tokens_here
    vocab_count = lax.axis_size("vocab")
    seq_count = lax.axis_size("seq")
    vmem = pl.BlockSpec(memory_space=pltpu.VMEM)
    dma = pltpu.SemaphoreType.DMA
    return pl.pallas_call(
        head_kernel,
        out_shape=(
            jax.ShapeDtypeStruct((docs_count, entries), jnp.float32),
            jax.ShapeDtypeStruct((docs_count, tokens_here, width), jnp.bfloat16),
        ),
        in_specs=[
            pl.BlockSpec(memory_space=pltpu.SMEM),
            vmem,
            pl.BlockSpec(memory_space=pl.ANY),
            vmem,
        ],
        out_specs=(vmem, vmem),
        scratch_shapes=[
            pltpu.VMEM((width, entries), jnp.bfloat16),
            pltpu.VMEM((vocab_count, block_rows, width), jnp.bfloat16),
            pltpu.VMEM((vocab_count, block_rows, entries), jnp.float32),
            pltpu.VMEM((seq_count, docs_count, entries), jnp.float32),
            pltpu.VMEM((block_rows, entries), jnp.bfloat16),
            pltpu.VMEM((4, block_rows, width), jnp.bfloat16),
            pltpu.VMEM((4, block_rows, width), jnp.float32),
            pltpu.VMEM((4, block_rows, width), jnp.bfloat16),
            pltpu.VMEM((2, 4, block_rows, width), jnp.bfloat16),
            pltpu.VMEM((4, block_rows, width), jnp.bfloat16),
            pltpu.VMEM((tokens_here, width), jnp.bfloat16),
            dma,
            dma,
            dma((vocab_count, 4, 2)),
            dma((vocab_count, 2)),
            dma((seq_count,)),
            dma((seq_count,)),
            dma((4, 2)),
            dma((4, 2)),
            dma((4, 2)),
            dma((2, 4, 2)),
            dma,
            dma,
        ],
        compiler_params=pltpu.CompilerParams(
            collective_id=2, has_side_effects=True, vmem_limit_bytes=48 * 1024 * 1024
        ),
    )(doc_lengths, hidden.reshape(block_rows, width), head_weight, head_bias[None, :])


def attend_blocks(
    queries, key_vectors, value_vectors, residual, norm_gain, doc_lengths
):
    tokens_here = queries.shape[0]
    docs_count = queries.shape[1]
    vocab_count = lax.axis_size("vocab")
    query_heads, key_heads, value_heads = (
        lax.all_to_all(queries, "seq", split_axis=2, concat_axis=0, tiled=True),
        lax.all_to_all(key_vectors, "seq", split_axis=2, concat_axis=0, tiled=True),
        lax.all_to_all(value_vectors, "seq", split_axis=2, concat_axis=0, tiled=True),
    )
    block_rows = query_heads.shape[0]
    local_width = query_heads.shape[2]
    local_heads = local_width // HEAD_DIM
    query_split = query_heads.reshape(block_rows, docs_count, local_heads, HEAD_DIM)
    within = jnp.arange(block_rows, dtype=jnp.int32)

    def attend_block(carry, block):
        highest, total, summed = carry
        key_block, value_block, shard = block
        key_split = key_block.reshape(block_rows, docs_count, local_heads, HEAD_DIM)
        value_split = value_block.reshape(block_rows, docs_count, local_heads, HEAD_DIM)
        key_place = (
            within // tokens_here * vocab_count + shard
        ) * tokens_here + within % tokens_here
        allowed = (key_place[None, :] < doc_lengths[:, None])[:, None, None, :]
        scores = jnp.einsum(
            "qbhe,kbhe->bhqk", query_split, key_split, preferred_element_type=jnp.float32
        ) / math.sqrt(HEAD_DIM)
        block_top = jnp.max(jnp.where(allowed, scores, -1e30), axis=3)
        new_top = jnp.maximum(highest, block_top)
        weights = jnp.where(allowed, jnp.exp(scores - new_top[..., None]), 0.0)
        shrink = jnp.exp(highest - new_top)
        total = total * shrink + jnp.sum(weights, axis=3)
        added = jnp.einsum(
            "bhqk,kbhe->qbhe",
            weights.astype(jnp.bfloat16),
            value_split,
            preferred_element_type=jnp.float32,
        )
        summed = summed * jnp.transpose(shrink, (2, 0, 1))[..., None] + added
        return ((new_top, total, summed), None)

    initial = (
        jnp.full((docs_count, local_heads, block_rows), -1e30, jnp.float32),
        jnp.zeros((docs_count, local_heads, block_rows), jnp.float32),
        jnp.zeros((block_rows, docs_count, local_heads, HEAD_DIM), jnp.float32),
    )
    carry = initial
    key_piece = lax.all_gather(key_heads, "vocab", axis=0, tiled=True)
    value_piece = lax.all_gather(value_heads, "vocab", axis=0, tiled=True)
    count = key_piece.shape[0] // block_rows
    key_blocks = key_piece.reshape(count, block_rows, docs_count, local_width)
    value_blocks = value_piece.reshape(count, block_rows, docs_count, local_width)
    shards = jnp.arange(count, dtype=jnp.int32)
    carry, unused = lax.scan(attend_block, carry, (key_blocks, value_blocks, shards))
    highest, total, summed = carry
    attended = (
        (summed / jnp.transpose(total, (2, 0, 1))[..., None])
        .reshape(block_rows, docs_count, local_width)
        .astype(jnp.bfloat16)
    )
    returned = lax.all_to_all(attended, "seq", split_axis=0, concat_axis=2, tiled=True)
    combined = residual.astype(jnp.float32) + returned.astype(jnp.float32)
    inv_rms = lax.rsqrt(jnp.mean(combined * combined, axis=2, keepdims=True) + epsilon)
    hidden = (combined * inv_rms * norm_gain).astype(jnp.bfloat16)
    return hidden


def local(
    queries, key_vectors, value_vectors, residual, norm_gain, head_weight, head_bias, doc_lengths
):
    tokens_here = queries.shape[0]
    docs_count = queries.shape[1]
    vocab_count = lax.axis_size("vocab")
    seq_at = lax.axis_index("seq")
    heads = queries.shape[2] // HEAD_DIM
    if vocab_count == 8 and lax.axis_size("seq") * vocab_count == docs_count * heads:
        hidden = attend_all(
            queries, key_vectors, value_vectors, residual, norm_gain, doc_lengths
        )
        pooled, gradient = head_all(hidden, head_weight, head_bias, doc_lengths)
        return (pooled, gradient.transpose(1, 0, 2))
    hidden = attend_blocks(
        queries, key_vectors, value_vectors, residual, norm_gain, doc_lengths
    )
    arrived = lax.all_gather(hidden, "vocab", axis=0, tiled=True)
    row_count = arrived.shape[0]
    flattened = jnp.dot(
        arrived.reshape(row_count * docs_count, arrived.shape[2]),
        head_weight,
        preferred_element_type=jnp.float32,
    )
    logits = flattened.reshape(row_count, docs_count, head_weight.shape[1]) + head_bias
    gathered_rows = logits.shape[0]
    row_index = jnp.arange(gathered_rows, dtype=jnp.int32)
    position = (
        seq_at * vocab_count + row_index // tokens_here
    ) * tokens_here + row_index % tokens_here
    row_allowed = position[:, None] < doc_lengths[None, :]
    saturated = jnp.log1p(jnp.maximum(logits, 0.0))
    boosted = jnp.where(row_allowed[:, :, None], jnp.exp(sharpness * saturated), 0.0)
    partial_sums = jnp.sum(boosted, axis=0)
    lengths_float = doc_lengths[:, None].astype(jnp.float32)
    totals = lax.psum(partial_sums, "seq")
    pooled = jnp.log(totals / lengths_float) / sharpness
    coefficient = 2.0 * flops_weight / docs_count * jnp.mean(pooled, axis=0)[None, :] / totals
    derivative = jnp.where(logits > 0.0, 1.0 / (1.0 + jnp.maximum(logits, 0.0)), 0.0)
    dlogits = (coefficient[None, :, :] * boosted * derivative).astype(jnp.bfloat16)
    flattened = lax.dot_general(
        dlogits.reshape(gathered_rows * docs_count, dlogits.shape[2]),
        head_weight,
        (((1,), (1,)), ((), ())),
        preferred_element_type=jnp.float32,
    )
    own_rows = lax.psum_scatter(
        flattened.reshape(gathered_rows, docs_count, head_weight.shape[0]).astype(jnp.bfloat16),
        "vocab",
        scatter_dimension=0,
        tiled=True,
    )
    return (pooled, own_rows)


def solution(mesh):
    in_specs = (
        P(("seq", "vocab"), None, None),
        P(("seq", "vocab"), None, None),
        P(("seq", "vocab"), None, None),
        P(("seq", "vocab"), None, None),
        P(),
        P(None, "vocab"),
        P("vocab"),
        P(),
    )
    out_specs = (P(None, "vocab"), P(("seq", "vocab"), None, None))
    return jax.shard_map(local, mesh=mesh, in_specs=in_specs, out_specs=out_specs, check_vma=False)
```

```python
import functools
import math

import jax
import jax.numpy as jnp
from jax import lax
from jax.experimental import pallas as pl
from jax.experimental.pallas import tpu as pltpu
from jax.sharding import PartitionSpec as P

HEAD_DIM = 128


sharpness = 8.0
flops_weight = 500.0
epsilon = 1e-05


def place(device, vocab_count):
    return (device // vocab_count, device % vocab_count)


def meet(devices, me, vocab_count):
    barrier = pltpu.get_barrier_semaphore()

    @pl.loop(1, devices)
    def greet(step):
        pl.semaphore_signal(
            barrier,
            inc=1,
            device_id=place((me + step) % devices, vocab_count),
            device_id_type=pl.DeviceIdType.MESH,
        )

    pl.semaphore_wait(barrier, devices - 1)


def attend_kernel(
    devices,
    vocab_count,
    heads,
    chunk_blocks,
    lengths_ref,
    packed_ref,
    residual_ref,
    gain_ref,
    hidden_ref,
    arrived,
    attended,
    returned,
    send_sem,
    recv_sem,
    back_send_sem,
    back_recv_sem,
    own_sem,
):
    me = lax.axis_index("seq") * vocab_count + lax.axis_index("vocab")
    docs_count, tokens_here, _ = hidden_ref.shape
    chunk = chunk_blocks * tokens_here
    length = devices * tokens_here
    meet(devices, me, vocab_count)

    def outgoing(other, source):
        return pltpu.make_async_remote_copy(
            src_ref=packed_ref.at[other],
            dst_ref=arrived.at[source],
            send_sem=send_sem.at[other],
            recv_sem=recv_sem.at[source],
            device_id=place(other, vocab_count),
            device_id_type=pl.DeviceIdType.MESH,
        )

    def back(other, source):
        return pltpu.make_async_remote_copy(
            src_ref=attended.at[other],
            dst_ref=returned.at[source],
            send_sem=back_send_sem.at[other],
            recv_sem=back_recv_sem.at[source],
            device_id=place(other, vocab_count),
            device_id_type=pl.DeviceIdType.MESH,
        )

    @pl.loop(1, devices)
    def send(step):
        outgoing((me + step) % devices, me).start()

    own = pltpu.make_async_copy(packed_ref.at[me], arrived.at[me], own_sem)
    own.start()
    own.wait()

    @pl.loop(1, devices)
    def receive(step):
        other = (me + step) % devices
        outgoing(other, other).wait_recv()

    real = lengths_ref[me // heads]
    slots = lax.broadcasted_iota(jnp.int32, (1, length), 1)
    bias = jnp.where(slots < real, 0.0, -1e30)
    factor = math.log2(math.e) / math.sqrt(HEAD_DIM)
    count = devices // chunk_blocks

    @pl.loop(0, count)
    def attend(step):
        first = ((step + me // chunk_blocks) % count) * chunk_blocks
        query = arrived[pl.ds(first, chunk_blocks), 0].reshape(chunk, HEAD_DIM)
        keys = arrived[:, 1].reshape(length, HEAD_DIM)
        scores = lax.dot_general(
            query, keys, (((1,), (1,)), ((), ())), preferred_element_type=jnp.float32
        )
        scores = scores + bias
        top = jnp.max(scores, axis=1, keepdims=True)
        weights = jnp.exp2((scores - top) * factor)
        total = jnp.sum(weights, axis=1, keepdims=True)
        values = arrived[:, 2].reshape(length, HEAD_DIM)
        summed = jnp.dot(
            weights.astype(jnp.bfloat16), values, preferred_element_type=jnp.float32
        )
        result = (summed / total).astype(jnp.bfloat16)
        attended[pl.ds(first, chunk_blocks)] = result.reshape(
            chunk_blocks, tokens_here, HEAD_DIM
        )
        for block in range(chunk_blocks):
            other = first + block

            @pl.when(other != me)
            def give():
                back(other, me).start()

    keep = pltpu.make_async_copy(attended.at[me], returned.at[me], own_sem)
    keep.start()
    keep.wait()

    @pl.loop(1, devices)
    def finish(step):
        other = (me + step) % devices
        back(other, other).wait_recv()

    for doc in range(docs_count):
        combined = []
        squares = jnp.zeros((tokens_here, HEAD_DIM), jnp.float32)
        for head in range(heads):
            term = residual_ref[doc, :, head * HEAD_DIM : (head + 1) * HEAD_DIM].astype(
                jnp.float32
            ) + returned[doc * heads + head].astype(jnp.float32)
            squares = squares + term * term
            combined.append(term)
        mean = jnp.sum(squares, axis=1, keepdims=True) / (heads * HEAD_DIM)
        inv_rms = lax.rsqrt(mean + epsilon)
        for head in range(heads):
            at = slice(head * HEAD_DIM, (head + 1) * HEAD_DIM)
            hidden_ref[doc, :, at] = (combined[head] * inv_rms * gain_ref[:, at]).astype(
                jnp.bfloat16
            )

    @pl.loop(1, devices)
    def drain(step):
        other = (me + step) % devices
        outgoing(other, me).wait_send()
        back(other, me).wait_send()


def attend_all(queries, key_vectors, value_vectors, residual, norm_gain, doc_lengths):
    tokens_here, docs_count, width = queries.shape
    heads = width // HEAD_DIM
    vocab_count = lax.axis_size("vocab")
    devices = lax.axis_size("seq") * vocab_count
    packed = jnp.stack([queries, key_vectors, value_vectors])
    packed = packed.reshape(3, tokens_here, docs_count, heads, HEAD_DIM)
    packed = packed.transpose(2, 3, 0, 1, 4).reshape(devices, 3, tokens_here, HEAD_DIM)
    vmem = pl.BlockSpec(memory_space=pltpu.VMEM)
    return pl.pallas_call(
        functools.partial(attend_kernel, devices, vocab_count, heads, 4),
        out_shape=jax.ShapeDtypeStruct((docs_count, tokens_here, width), jnp.bfloat16),
        in_specs=[pl.BlockSpec(memory_space=pltpu.SMEM), vmem, vmem, vmem],
        out_specs=vmem,
        scratch_shapes=[
            pltpu.VMEM((devices, 3, tokens_here, HEAD_DIM), jnp.bfloat16),
            pltpu.VMEM((devices, tokens_here, HEAD_DIM), jnp.bfloat16),
            pltpu.VMEM((devices, tokens_here, HEAD_DIM), jnp.bfloat16),
            pltpu.SemaphoreType.DMA((devices,)),
            pltpu.SemaphoreType.DMA((devices,)),
            pltpu.SemaphoreType.DMA((devices,)),
            pltpu.SemaphoreType.DMA((devices,)),
            pltpu.SemaphoreType.DMA,
        ],
        compiler_params=pltpu.CompilerParams(
            collective_id=1, has_side_effects=True, vmem_limit_bytes=40 * 1024 * 1024
        ),
    )(doc_lengths, packed, residual.transpose(1, 0, 2), norm_gain[None, :])


def turn(z, step):
    return (3 * (1 - lax.div(z, 2)), lax.rem(2 + 3 * z, 5), 1 + lax.rem(z, 2), z)[step]


def head_kernel(
    lengths_ref,
    hidden_ref,
    weight_hbm,
    bias_ref,
    pooled_ref,
    grad_ref,
    weight,
    rows,
    logits,
    partials,
    slopes,
    across,
    kept,
    from_side,
    from_line,
    passing,
    from_partner,
    weight_sem,
    own_sem,
    row_send,
    row_recv,
    sum_send,
    sum_recv,
    side_send,
    side_recv,
    line_send,
    line_recv,
    partner_send,
    partner_recv,
):
    seq_at = lax.axis_index("seq")
    vocab_at = lax.axis_index("vocab")
    z, x = lax.div(vocab_at, 2), lax.rem(vocab_at, 2)
    docs_count, tokens_here, width = grad_ref.shape
    block_rows = docs_count * tokens_here
    entries = weight.shape[1]
    seq_count = partials.shape[0]
    up, down, side = (seq_at, vocab_at + 2), (seq_at, vocab_at - 2), (seq_at, z * 2 + 1 - x)
    partner_row = z + 1 - 2 * lax.rem(z, 2)
    partner = (seq_at, partner_row * 2 + x)
    mesh_id = pl.DeviceIdType.MESH

    load = pltpu.make_async_copy(weight_hbm, weight, weight_sem)
    load.start()
    own = pltpu.make_async_copy(hidden_ref, rows.at[vocab_at], own_sem)
    own.start()

    barrier = pltpu.get_barrier_semaphore()
    pl.semaphore_signal(barrier, inc=1, device_id=side, device_id_type=mesh_id)
    for step in range(1, seq_count):
        mate = (lax.rem(seq_at + step, seq_count), vocab_at)
        pl.semaphore_signal(barrier, inc=1, device_id=mate, device_id_type=mesh_id)

    @pl.when(z < 3)
    def greet_up():
        pl.semaphore_signal(barrier, inc=1, device_id=up, device_id_type=mesh_id)

    @pl.when(z > 0)
    def greet_down():
        pl.semaphore_signal(barrier, inc=1, device_id=down, device_id_type=mesh_id)

    pl.semaphore_wait(barrier, seq_count + lax.div(z + 3, 4) + lax.div(6 - z, 4))

    def row_copy(slot, way, half):
        part = rows.at[slot, pl.ds(half * tokens_here, tokens_here)]
        return pltpu.make_async_remote_copy(
            src_ref=part,
            dst_ref=part,
            send_sem=row_send.at[slot, way, half],
            recv_sem=row_recv.at[slot, half],
            device_id=(up, down, side, partner)[way],
            device_id_type=mesh_id,
        )

    def pass_rows(row, half, act):
        slot = row * 2 + x

        @pl.when(jnp.logical_and(row <= z, z < 3))
        def upward():
            act(row_copy(slot, 0, half))

        @pl.when(jnp.logical_and(row >= z, z > 0))
        def downward():
            act(row_copy(slot, 1, half))

        if half == 0:
            act(row_copy(slot, 2, half))
        else:

            @pl.when(row != partner_row)
            def sideways():
                act(row_copy(slot, 2, half))

    partials[seq_at] = jnp.zeros((docs_count, entries), jnp.float32)
    tile = 256

    def project(slot, docs=range(docs_count)):
        low = docs[0] * tokens_here
        block = rows[slot, low : low + len(docs) * tokens_here]

        @pl.loop(0, entries // tile)
        def columns(step):
            at = pl.ds(pl.multiple_of(step * tile, tile), tile)
            found = (
                jnp.dot(block, weight[:, at], preferred_element_type=jnp.float32)
                + bias_ref[:, at]
            )
            first = (seq_at * 8 + slot) * tokens_here
            place_of = first + lax.broadcasted_iota(jnp.int32, (tokens_here, tile), 0)
            for doc in docs:
                real = place_of < lengths_ref[doc]
                part = found[doc * tokens_here - low : (doc + 1) * tokens_here - low]
                base = 1.0 + jnp.maximum(part, 0.0)
                power = base * base
                power = power * power
                boosted = jnp.where(real, power * power, 0.0)
                total = jnp.sum(boosted, axis=0, keepdims=True)
                partials[seq_at, doc : doc + 1, at] = (
                    partials[seq_at, doc : doc + 1, at] + total
                )
                logits[slot, doc * tokens_here : (doc + 1) * tokens_here, at] = jnp.where(
                    real, part, 0.0
                )

    own.wait()
    for half in range(2):
        pass_rows(z, half, lambda copy: copy.start())
    load.wait()
    project(vocab_at)
    for step in range(1, 4):
        row, before = turn(z, 3 - step), turn(z, 4 - step)
        for half in range(2):
            row_copy(row * 2 + x, 2, half).wait_recv()
            pass_rows(row, half, lambda copy: copy.start())
        if step > 1:
            project(row * 2 + x)
        for half in range(2):
            row_copy(before * 2 + 1 - x, 2, half).wait_recv()
        if step == 1:
            row_copy(before * 2 + 1 - x, 3, 1).start()
            project(row * 2 + x)
        project(before * 2 + 1 - x)
    last = turn(z, 0) * 2 + 1 - x
    for half in range(2):
        row_copy(last, 2, half).wait_recv()
        project(last, range(half, half + 1))

    def sum_copy(step, source):
        return pltpu.make_async_remote_copy(
            src_ref=partials.at[seq_at],
            dst_ref=partials.at[source],
            send_sem=sum_send.at[step],
            recv_sem=sum_recv.at[source],
            device_id=(lax.rem(seq_at + step, seq_count), vocab_at),
            device_id_type=mesh_id,
        )

    for step in range(1, seq_count):
        sum_copy(step, seq_at).start()
    for step in range(1, seq_count):
        sum_copy(step, lax.rem(seq_at + step, seq_count)).wait_recv()
    totals = partials[0]
    for other in range(1, seq_count):
        totals = totals + partials[other]
    usage = jnp.zeros((1, entries), jnp.float32)
    for doc in range(docs_count):
        length = jnp.full((1, entries), lengths_ref[doc], jnp.int32).astype(jnp.float32)
        pooled = jnp.log(totals[doc : doc + 1] / length) / sharpness
        pooled_ref[doc : doc + 1, :] = pooled
        usage = usage + pooled
    usage = usage / docs_count
    coefficient = [
        2.0 * flops_weight / docs_count * usage / totals[doc : doc + 1]
        for doc in range(docs_count)
    ]

    def slope(slot):
        for doc in range(docs_count):
            part = logits[slot, doc * tokens_here : (doc + 1) * tokens_here]
            base = 1.0 + jnp.maximum(part, 0.0)
            square = base * base
            boosted_slope = square * square * (square * base)
            slopes[doc * tokens_here : (doc + 1) * tokens_here] = jnp.where(
                part > 0.0, coefficient[doc] * boosted_slope, 0.0
            ).astype(jnp.bfloat16)

    def gradient(slot, write):
        slope(slot)

        @pl.loop(0, width // tile)
        def features(step):
            at = pl.ds(pl.multiple_of(step * tile, tile), tile)
            write(
                at,
                lax.dot_general(
                    slopes[...],
                    weight[at, :],
                    (((1,), (1,)), ((), ())),
                    preferred_element_type=jnp.float32,
                ),
            )

    def side_copy(row, half):
        part = pl.ds(half * tokens_here, tokens_here)
        return pltpu.make_async_remote_copy(
            src_ref=across.at[row, part],
            dst_ref=from_side.at[row, part],
            send_sem=side_send.at[row, half],
            recv_sem=side_recv.at[row, half],
            device_id=side,
            device_id_type=mesh_id,
        )

    partner_copy = pltpu.make_async_remote_copy(
        src_ref=across.at[partner_row, pl.ds(tokens_here, tokens_here)],
        dst_ref=from_partner,
        send_sem=partner_send,
        recv_sem=partner_recv,
        device_id=partner,
        device_id_type=mesh_id,
    )

    def line_copy(row, way, half):
        part = pl.ds(half * tokens_here, tokens_here)
        return pltpu.make_async_remote_copy(
            src_ref=passing.at[row, part],
            dst_ref=from_line.at[way, row, part],
            send_sem=line_send.at[row, half],
            recv_sem=line_recv.at[way, row, half],
            device_id=(up, down)[way],
            device_id_type=mesh_id,
        )

    for step in range(4):
        row = turn(z, step)

        def write_across(at, value):
            across[row, :, at] = value.astype(jnp.bfloat16)

        gradient(row * 2 + 1 - x, write_across)
        side_copy(row, 0).start()
        if step < 3:

            @pl.when(row == partner_row)
            def by_line():
                partner_copy.start()

            @pl.when(row != partner_row)
            def by_side():
                side_copy(row, 1).start()

    for step in range(4):
        row = turn(z, step)

        def write_kept(at, value):
            kept[row, :, at] = value

        gradient(row * 2 + x, write_kept)
        if step == 0:
            partner_copy.wait_recv()
            late = pl.ds(tokens_here, tokens_here)
            across[z, late] = (
                across[z, late].astype(jnp.float32) + from_partner[...].astype(jnp.float32)
            ).astype(jnp.bfloat16)
            side_copy(z, 1).start()
        for half in range(2):
            part = pl.ds(half * tokens_here, tokens_here)

            @pl.when(jnp.logical_and(row >= z, z > 0))
            def from_below():
                line_copy(row, 0, half).wait_recv()
                kept[row, part] = kept[row, part] + from_line[0, row, part].astype(
                    jnp.float32
                )

            @pl.when(jnp.logical_and(row <= z, z < 3))
            def from_above():
                line_copy(row, 1, half).wait_recv()
                kept[row, part] = kept[row, part] + from_line[1, row, part].astype(
                    jnp.float32
                )

            def add_side():
                side_copy(row, half).wait_recv()
                kept[row, part] = kept[row, part] + from_side[row, part].astype(jnp.float32)

            if half == 0 or step == 3:
                add_side()
            else:
                pl.when(row != partner_row)(add_side)
            total = kept[row, part].astype(jnp.bfloat16)
            if step < 3:
                passing[row, part] = total

                @pl.when(row > z)
                def upward():
                    line_copy(row, 0, half).start()

                @pl.when(row < z)
                def downward():
                    line_copy(row, 1, half).start()

            else:
                grad_ref[half] = total

    for step in range(4):
        row = turn(z, step)
        for half in range(2):
            pass_rows(row, half, lambda copy: copy.wait_send())
            if step < 3:
                line_copy(row, 0, half).wait_send()
        side_copy(row, 0).wait_send()

        @pl.when(row != partner_row)
        def sent():
            side_copy(row, 1).wait_send()

    partner_copy.wait_send()
    row_copy(z * 2 + 1 - x, 3, 1).wait_send()
    for step in range(1, seq_count):
        sum_copy(step, seq_at).wait_send()


def head_all(hidden, head_weight, head_bias, doc_lengths):
    docs_count, tokens_here, width = hidden.shape
    entries = head_weight.shape[1]
    block_rows = docs_count * tokens_here
    vocab_count = lax.axis_size("vocab")
    seq_count = lax.axis_size("seq")
    vmem = pl.BlockSpec(memory_space=pltpu.VMEM)
    dma = pltpu.SemaphoreType.DMA
    return pl.pallas_call(
        head_kernel,
        out_shape=(
            jax.ShapeDtypeStruct((docs_count, entries), jnp.float32),
            jax.ShapeDtypeStruct((docs_count, tokens_here, width), jnp.bfloat16),
        ),
        in_specs=[
            pl.BlockSpec(memory_space=pltpu.SMEM),
            vmem,
            pl.BlockSpec(memory_space=pl.ANY),
            vmem,
        ],
        out_specs=(vmem, vmem),
        scratch_shapes=[
            pltpu.VMEM((width, entries), jnp.bfloat16),
            pltpu.VMEM((vocab_count, block_rows, width), jnp.bfloat16),
            pltpu.VMEM((vocab_count, block_rows, entries), jnp.float32),
            pltpu.VMEM((seq_count, docs_count, entries), jnp.float32),
            pltpu.VMEM((block_rows, entries), jnp.bfloat16),
            pltpu.VMEM((4, block_rows, width), jnp.bfloat16),
            pltpu.VMEM((4, block_rows, width), jnp.float32),
            pltpu.VMEM((4, block_rows, width), jnp.bfloat16),
            pltpu.VMEM((2, 4, block_rows, width), jnp.bfloat16),
            pltpu.VMEM((4, block_rows, width), jnp.bfloat16),
            pltpu.VMEM((tokens_here, width), jnp.bfloat16),
            dma,
            dma,
            dma((vocab_count, 4, 2)),
            dma((vocab_count, 2)),
            dma((seq_count,)),
            dma((seq_count,)),
            dma((4, 2)),
            dma((4, 2)),
            dma((4, 2)),
            dma((2, 4, 2)),
            dma,
            dma,
        ],
        compiler_params=pltpu.CompilerParams(
            collective_id=2, has_side_effects=True, vmem_limit_bytes=48 * 1024 * 1024
        ),
    )(doc_lengths, hidden.reshape(block_rows, width), head_weight, head_bias[None, :])


def attend_blocks(
    queries, key_vectors, value_vectors, residual, norm_gain, doc_lengths
):
    tokens_here = queries.shape[0]
    docs_count = queries.shape[1]
    vocab_count = lax.axis_size("vocab")
    query_heads, key_heads, value_heads = (
        lax.all_to_all(queries, "seq", split_axis=2, concat_axis=0, tiled=True),
        lax.all_to_all(key_vectors, "seq", split_axis=2, concat_axis=0, tiled=True),
        lax.all_to_all(value_vectors, "seq", split_axis=2, concat_axis=0, tiled=True),
    )
    block_rows = query_heads.shape[0]
    local_width = query_heads.shape[2]
    local_heads = local_width // HEAD_DIM
    query_split = query_heads.reshape(block_rows, docs_count, local_heads, HEAD_DIM)
    within = jnp.arange(block_rows, dtype=jnp.int32)

    def attend_block(carry, block):
        highest, total, summed = carry
        key_block, value_block, shard = block
        key_split = key_block.reshape(block_rows, docs_count, local_heads, HEAD_DIM)
        value_split = value_block.reshape(block_rows, docs_count, local_heads, HEAD_DIM)
        key_place = (
            within // tokens_here * vocab_count + shard
        ) * tokens_here + within % tokens_here
        allowed = (key_place[None, :] < doc_lengths[:, None])[:, None, None, :]
        scores = jnp.einsum(
            "qbhe,kbhe->bhqk", query_split, key_split, preferred_element_type=jnp.float32
        ) / math.sqrt(HEAD_DIM)
        block_top = jnp.max(jnp.where(allowed, scores, -1e30), axis=3)
        new_top = jnp.maximum(highest, block_top)
        weights = jnp.where(allowed, jnp.exp(scores - new_top[..., None]), 0.0)
        shrink = jnp.exp(highest - new_top)
        total = total * shrink + jnp.sum(weights, axis=3)
        added = jnp.einsum(
            "bhqk,kbhe->qbhe",
            weights.astype(jnp.bfloat16),
            value_split,
            preferred_element_type=jnp.float32,
        )
        summed = summed * jnp.transpose(shrink, (2, 0, 1))[..., None] + added
        return ((new_top, total, summed), None)

    initial = (
        jnp.full((docs_count, local_heads, block_rows), -1e30, jnp.float32),
        jnp.zeros((docs_count, local_heads, block_rows), jnp.float32),
        jnp.zeros((block_rows, docs_count, local_heads, HEAD_DIM), jnp.float32),
    )
    carry = initial
    key_piece = lax.all_gather(key_heads, "vocab", axis=0, tiled=True)
    value_piece = lax.all_gather(value_heads, "vocab", axis=0, tiled=True)
    count = key_piece.shape[0] // block_rows
    key_blocks = key_piece.reshape(count, block_rows, docs_count, local_width)
    value_blocks = value_piece.reshape(count, block_rows, docs_count, local_width)
    shards = jnp.arange(count, dtype=jnp.int32)
    carry, unused = lax.scan(attend_block, carry, (key_blocks, value_blocks, shards))
    highest, total, summed = carry
    attended = (
        (summed / jnp.transpose(total, (2, 0, 1))[..., None])
        .reshape(block_rows, docs_count, local_width)
        .astype(jnp.bfloat16)
    )
    returned = lax.all_to_all(attended, "seq", split_axis=0, concat_axis=2, tiled=True)
    combined = residual.astype(jnp.float32) + returned.astype(jnp.float32)
    inv_rms = lax.rsqrt(jnp.mean(combined * combined, axis=2, keepdims=True) + epsilon)
    hidden = (combined * inv_rms * norm_gain).astype(jnp.bfloat16)
    return hidden


def local(
    queries, key_vectors, value_vectors, residual, norm_gain, head_weight, head_bias, doc_lengths
):
    tokens_here = queries.shape[0]
    docs_count = queries.shape[1]
    vocab_count = lax.axis_size("vocab")
    seq_at = lax.axis_index("seq")
    heads = queries.shape[2] // HEAD_DIM
    if vocab_count == 8 and lax.axis_size("seq") * vocab_count == docs_count * heads:
        hidden = attend_all(
            queries, key_vectors, value_vectors, residual, norm_gain, doc_lengths
        )
        pooled, gradient = head_all(hidden, head_weight, head_bias, doc_lengths)
        return (pooled, gradient.transpose(1, 0, 2))
    hidden = attend_blocks(
        queries, key_vectors, value_vectors, residual, norm_gain, doc_lengths
    )
    arrived = lax.all_gather(hidden, "vocab", axis=0, tiled=True)
    row_count = arrived.shape[0]
    flattened = jnp.dot(
        arrived.reshape(row_count * docs_count, arrived.shape[2]),
        head_weight,
        preferred_element_type=jnp.float32,
    )
    logits = flattened.reshape(row_count, docs_count, head_weight.shape[1]) + head_bias
    gathered_rows = logits.shape[0]
    row_index = jnp.arange(gathered_rows, dtype=jnp.int32)
    position = (
        seq_at * vocab_count + row_index // tokens_here
    ) * tokens_here + row_index % tokens_here
    row_allowed = position[:, None] < doc_lengths[None, :]
    saturated = jnp.log1p(jnp.maximum(logits, 0.0))
    boosted = jnp.where(row_allowed[:, :, None], jnp.exp(sharpness * saturated), 0.0)
    partial_sums = jnp.sum(boosted, axis=0)
    lengths_float = doc_lengths[:, None].astype(jnp.float32)
    totals = lax.psum(partial_sums, "seq")
    pooled = jnp.log(totals / lengths_float) / sharpness
    coefficient = 2.0 * flops_weight / docs_count * jnp.mean(pooled, axis=0)[None, :] / totals
    derivative = jnp.where(logits > 0.0, 1.0 / (1.0 + jnp.maximum(logits, 0.0)), 0.0)
    dlogits = (coefficient[None, :, :] * boosted * derivative).astype(jnp.bfloat16)
    flattened = lax.dot_general(
        dlogits.reshape(gathered_rows * docs_count, dlogits.shape[2]),
        head_weight,
        (((1,), (1,)), ((), ())),
        preferred_element_type=jnp.float32,
    )
    own_rows = lax.psum_scatter(
        flattened.reshape(gathered_rows, docs_count, head_weight.shape[0]).astype(jnp.bfloat16),
        "vocab",
        scatter_dimension=0,
        tiled=True,
    )
    return (pooled, own_rows)


def solution(mesh):
    in_specs = (
        P(("seq", "vocab"), None, None),
        P(("seq", "vocab"), None, None),
        P(("seq", "vocab"), None, None),
        P(("seq", "vocab"), None, None),
        P(),
        P(None, "vocab"),
        P("vocab"),
        P(),
    )
    out_specs = (P(None, "vocab"), P(("seq", "vocab"), None, None))
    return jax.shard_map(local, mesh=mesh, in_specs=in_specs, out_specs=out_specs, check_vma=False)
```
